256 devices in a mesh: prompt: 16 (over z, core), sample: 16 (over x, y).
Axes of the slice: x: 4, y: 4, z: 8, core: 2. Of those that a mesh axis runs over, the one named last changes fastest.
Arguments:
- prompt_latent: bfloat16 [16, 73728], P('prompt', 'sample'), may hold values from -8 to 8
- resp_latent: bfloat16 [16, 1179648], P('prompt', 'sample'), may hold values from -6 to 6
- queries: bfloat16 [16, 2048, 12288], P('prompt', 'sample'), may hold values from -300 to 300
- d_attended: bfloat16 [16, 2048, 8192], P('prompt', 'sample'), may hold values from -6 to 6
- w_kv: bfloat16 [512, 16384], P(None, 'prompt'), may hold values from -0.25 to 0.25
- seg_ids: int32 [16, 2048], P('prompt', 'sample'), may hold values from 0 to 8, as said below
- live: int32 [16, 16], P('prompt', 'sample'), may hold values from 32 to 128, as said below
Outputs:
- attended: bfloat16 [16, 2048, 8192], P('prompt', 'sample')
- d_queries: bfloat16 [16, 2048, 12288], P('prompt', 'sample')
- d_prompt_latent: bfloat16 [16, 73728], P('prompt', 'sample')
- d_resp_latent: bfloat16 [16, 1179648], P('prompt', 'sample')
The draws below stay inside these ranges and needn't reach their ends.
Inputs may be any that keep to these rules, and one draw needn't show every extreme that they name: `seg_ids`: nondecreasing along each device's 128 slots, 0 at its first slot, rising by one at each of exactly 8 response starts; equal values mark one response. In every group some device has all 128 slots live.
All inputs are finite; a program needn't handle non-finite values.
Results may differ from the reference program's by a relative error of at most 0.02.
Values may be sent and summed in bfloat16 or wider, within the bound.
No kernel may reach another device: no remote copies, remote signals or barrier semaphores. Data moves between devices by JAX's collectives and lax.ppermute only.
A program may use at most 192 MiB of HBM per device.

```python
import jax
import jax.numpy as jnp
from jax import lax

DC = 512
DR = 64
DN = 128
DV = 128
H = 64
RESP = 128
GROUPS = 16
SAMPLES = 16
PROMPT = 128
RESP_ALL = 2048
DL = 576
DQ = 192


def rope_base(key, spread):
    return spread * jax.random.truncated_normal(key, -3.2, 3.2, (GROUPS, PROMPT, DR), jnp.float32)


def draw_prompt_latent(key, part):
    base = rope_base(key, 1.25)
    key = jax.random.fold_in(key, 11)
    first, second = jax.random.split(key)
    nope = jax.random.truncated_normal(first, -3.2, 3.2, (GROUPS, PROMPT, DC), jnp.float32)
    rising = jnp.exp(jnp.log(2.5) * jnp.arange(PROMPT, dtype=jnp.float32) / max(PROMPT - 1, 1))
    jitter = jnp.exp(jax.random.uniform(second, (GROUPS, PROMPT, 1), jnp.float32, -0.2, 0.0))
    nope = nope * rising[None, :, None] * jitter
    return jnp.concatenate([nope, base], axis=-1).reshape(GROUPS, PROMPT * DL).astype(jnp.bfloat16)


def draw_queries(key, part):
    key = jax.random.fold_in(key, 23)
    first = jax.random.fold_in(key, 0)
    shape = (GROUPS, RESP_ALL, H, DQ)
    values = 2.0 * jax.random.truncated_normal(first, -6.0, 6.0, shape, jnp.float32)
    return values.reshape(GROUPS, RESP_ALL, H * DQ).astype(jnp.bfloat16)


def draw_seg_ids(key, part):
    key = jax.random.fold_in(key, 41)
    count = max(RESP // 16, 2)
    position = jnp.arange(RESP, dtype=jnp.int32)
    scores = jax.random.randint(key, (GROUPS, SAMPLES, RESP), 0, 2 ** 19) * RESP + position[None, None, :]
    scores = jnp.where(position[None, None, :] == 0, jnp.int32(2 ** 31 - 1), scores)
    order = jnp.argsort(scores, axis=-1, stable=True)
    rank = jnp.argsort(order, axis=-1, stable=True)
    starts = (rank < count).astype(jnp.int32)
    return jnp.cumsum(starts, axis=-1).reshape(GROUPS, RESP_ALL).astype(jnp.int32)


def draw_live(key, part):
    key = jax.random.fold_in(key, 37)
    first, second = jax.random.split(key)
    counts = jax.random.randint(first, (GROUPS, SAMPLES), RESP // 4, RESP + 1)
    full = jax.random.randint(second, (GROUPS, 1), 0, SAMPLES)
    return jnp.where(jnp.arange(SAMPLES)[None, :] == full, RESP, counts).astype(jnp.int32)


def shard_levels(key, extent, shards, smallest, largest):
    gain = 1.0
    for axis_at, shards_of in shards:
        draws = jax.random.uniform(jax.random.fold_in(jax.random.fold_in(key, 6), axis_at), (shards_of,), jnp.float32, smallest / len(shards), largest / len(shards))
        gain = gain * jnp.repeat(jnp.exp(draws), extent[axis_at] // shards_of).reshape((-1,) + (1,) * (len(extent) - 1 - axis_at))
    return gain


def noise(stream_key, extent, scale, most, pieces=(), kind=jnp.bfloat16):
    drawn = jax.random.normal(stream_key, extent, jnp.float32) * scale
    if len(pieces) > 0:
        drawn = shard_levels(stream_key, extent, pieces, -0.22, 0.18) * drawn
    return jnp.clip(drawn, min=-most, max=most).astype(kind)


def setup_inputs(seed: int = 0) -> dict:
    key_of = jax.random.split(jax.random.key(seed), 8)
    return {
        "prompt_latent": draw_prompt_latent(jax.random.fold_in(key_of[7], 71), 0),
        "resp_latent": noise(key_of[1], (GROUPS, RESP_ALL * DL), 1.0, 6.0, ((0, 16), (1, 16))),
        "queries": draw_queries(jax.random.fold_in(key_of[7], 71), 0),
        "d_attended": noise(key_of[3], (GROUPS, RESP_ALL, H * DV), 1.0, 6.0, ((0, 16), (1, 16))),
        "w_kv": noise(key_of[4], (DC, H * (DN + DV)), DC ** -0.5, 0.25, ((1, 16),)),
        "seg_ids": draw_seg_ids(jax.random.fold_in(key_of[7], 71), 0),
        "live": draw_live(jax.random.fold_in(key_of[7], 71), 0),
    }


def attend(queries, keys_values, key_rope, seg_ids, live_count, d_out, w_kv):
    resp = queries.shape[0]
    total = keys_values.shape[0]
    prompt_rows = total - resp
    scale = 1.0 / (DQ ** 0.5)
    query3 = queries.reshape(resp, H, DQ).astype(jnp.float32)
    query_nope = query3[:, :, :DN]
    query_rope = query3[:, :, DN:]
    pairs = keys_values.reshape(total, H, DN + DV).astype(jnp.float32)
    keys = pairs[:, :, :DN]
    values = pairs[:, :, DN:]
    rope = key_rope.astype(jnp.float32)
    scores = jnp.einsum("ihd,jhd->hij", query_nope, keys) + jnp.einsum("ihd,jd->hij", query_rope, rope)
    scores = scores * scale
    position = jnp.arange(resp, dtype=jnp.int32)
    resp_ok = (seg_ids[None, :] == seg_ids[:, None]) & (position[None, :] <= position[:, None]) & (position[None, :] < live_count)
    allowed = jnp.concatenate([jnp.ones((resp, prompt_rows), bool), resp_ok], axis=1)
    query_live = position < live_count
    masked = jnp.where(allowed[None], scores, jnp.float32(-1e30))
    top = jnp.max(masked, axis=-1, keepdims=True)
    expd = jnp.where(allowed[None], jnp.exp(masked - top), jnp.float32(0.0))
    weights = expd / jnp.sum(expd, axis=-1, keepdims=True)
    weights = jnp.where(query_live[None, :, None], weights, jnp.float32(0.0))
    weights_b = weights.astype(jnp.bfloat16)
    weights_f = weights_b.astype(jnp.float32)
    attended = jnp.einsum("hij,jhd->ihd", weights_f, values).astype(jnp.bfloat16).reshape(resp, H * DV)
    grad = jnp.where(query_live[:, None, None], d_out.reshape(resp, H, DV), jnp.zeros((), d_out.dtype))
    grad_f = grad.astype(jnp.float32)
    d_weights = jnp.einsum("ihd,jhd->hij", grad_f, values)
    delta = jnp.sum(weights * d_weights, axis=-1, keepdims=True)
    d_scores = (weights * (d_weights - delta) * scale).astype(jnp.bfloat16).astype(jnp.float32)
    dq_nope = jnp.einsum("hij,jhd->ihd", d_scores, keys)
    dq_rope = jnp.einsum("hij,jd->ihd", d_scores, rope)
    d_queries = jnp.concatenate([dq_nope, dq_rope], axis=-1).astype(jnp.bfloat16).reshape(resp, H * DQ)
    d_keys = jnp.einsum("hij,ihd->jhd", d_scores, query_nope).astype(jnp.bfloat16)
    d_values = jnp.einsum("hij,ihd->jhd", weights_f, grad_f).astype(jnp.bfloat16)
    d_pairs = jnp.concatenate([d_keys, d_values], axis=-1).reshape(total, H * (DN + DV))
    d_rope = jnp.einsum("hij,ihd->jd", d_scores, query_rope)
    latent_part = lax.dot_general(d_pairs, w_kv, (((1,), (1,)), ((), ())), preferred_element_type=jnp.float32)
    term = jnp.concatenate([latent_part, d_rope], axis=1)
    return attended, d_queries, term


def reference(prompt_latent, resp_latent, queries, d_attended, w_kv, seg_ids, live):
    def group(inputs):
        prompt_flat, resp_flat, query_g, dout_g, seg_g, live_g = inputs
        prompt_rows = prompt_flat.reshape(PROMPT, DL)
        resp_rows = resp_flat.reshape(SAMPLES, RESP, DL)
        kv_prompt = jnp.dot(prompt_rows[:, :DC], w_kv, preferred_element_type=jnp.float32).astype(jnp.bfloat16)

        def block(carry, inner):
            resp_b, query_b, dout_b, seg_b, live_b = inner
            kv_resp = jnp.dot(resp_b[:, :DC], w_kv, preferred_element_type=jnp.float32).astype(jnp.bfloat16)
            keys_values = jnp.concatenate([kv_prompt, kv_resp], axis=0)
            key_rope = jnp.concatenate([prompt_rows[:, DC:], resp_b[:, DC:]], axis=0)
            attended, d_queries, term = attend(query_b, keys_values, key_rope, seg_b, live_b, dout_b, w_kv)
            return carry + term[:PROMPT], (attended, d_queries, term[PROMPT:].astype(jnp.bfloat16))

        summed, outs = lax.scan(block, jnp.zeros((PROMPT, DL), jnp.float32),
                                (resp_rows, query_g.reshape(SAMPLES, RESP, H * DQ), dout_g.reshape(SAMPLES, RESP, H * DV),
                                 seg_g.reshape(SAMPLES, RESP), live_g))
        attended, d_queries, resp_terms = outs
        return (attended.reshape(RESP_ALL, H * DV), d_queries.reshape(RESP_ALL, H * DQ),
                summed.astype(jnp.bfloat16).reshape(PROMPT * DL), resp_terms.reshape(RESP_ALL * DL))

    attended, d_queries, d_prompt_latent, d_resp_latent = lax.map(
        group, (prompt_latent, resp_latent, queries, d_attended, seg_ids, live))
    return (attended, d_queries, d_prompt_latent, d_resp_latent)
```

```python
import functools
import jax
import jax.numpy as jnp
from jax import lax
from jax.experimental import pallas as pl
from jax.experimental.pallas import tpu as pltpu
from jax.sharding import PartitionSpec as P

DC = 512
DR = 64
DL = 576
DN = 128
DQ = 192
ROWS = 128
KEYS = 256
HEADS = 4
SCALE = 1.0 / DQ**0.5
LOG2E = 1.4426950408889634
F32 = jnp.float32
BF16 = jnp.bfloat16


def mm(a, b, ca, cb):
    return lax.dot_general(a, b, (((ca,), (cb,)), ((), ())), preferred_element_type=F32)


def attend_kernel(order_ref, lat_ref, rope_ref, bias_ref, alive_ref, w_ref, q_ref, g_ref, acc_in,
                  *rest):
    out_ref, dq_ref, acc_ref, kv_ref, dkv_ref = rest[-5:]

    @pl.when(pl.program_id(0) == 0)
    def _():
        acc_ref[...] = acc_in[...]

    w = w_ref[...].reshape(DC, HEADS * 256)
    kv_ref[...] = mm(lat_ref[...], w, 1, 0).astype(BF16)
    rope_even = rope_ref[:, :128]
    rope_odd = rope_ref[:, 128:]
    bias = bias_ref[...]
    alive = alive_ref[...]
    low = lax.broadcasted_iota(jnp.int32, (KEYS, 128), 1) < DR
    for pair in range(HEADS // 2):
        merged = None
        for odd in range(2):
            head = pair * 2 + odd
            at = pair * 384 + odd * 128
            q = q_ref[:, at : at + 256]
            g = g_ref[:, head * 128 : (head + 1) * 128]
            key = kv_ref[:, head * 256 : head * 256 + 128]
            value = kv_ref[:, head * 256 + 128 : (head + 1) * 256]
            if odd:
                turned = jnp.concatenate([key[:, DR:], key[:, :DR]], axis=1)
                zero = jnp.zeros_like(turned)
                key_row = jnp.concatenate(
                    [jnp.where(low, zero, turned), jnp.where(low, turned, rope_odd)], axis=1
                )
            else:
                key_row = jnp.concatenate([key, rope_even], axis=1)
            s = mm(key_row, q, 1, 1)
            s = jnp.concatenate([s[:ROWS], s[ROWS:] + bias], axis=0)
            top = jnp.max(s, axis=0, keepdims=True)
            e = jnp.exp2((s - top) * (SCALE * LOG2E))
            inv = alive / jnp.sum(e, axis=0, keepdims=True)
            a_b = (e * inv).astype(BF16)
            d_a = mm(value, g, 1, 1)
            delta = jnp.sum(e * d_a, axis=0, keepdims=True) * inv
            d_s = ((e * (d_a - delta)) * (inv * SCALE)).astype(BF16)
            out_ref[:, head * 128 : (head + 1) * 128] = mm(a_b, value, 0, 0).astype(BF16)
            d_q = mm(d_s, key_row, 0, 0)
            if odd:
                dq_ref[:, pair * 384 : pair * 384 + 128] = merged[:, :128].astype(BF16)
                dq_ref[:, pair * 384 + 128 : pair * 384 + 256] = (
                    merged[:, 128:] + d_q[:, :128]
                ).astype(BF16)
                dq_ref[:, pair * 384 + 256 : pair * 384 + 384] = d_q[:, 128:].astype(BF16)
            else:
                merged = d_q
            d_k = mm(d_s, q, 1, 0)
            d_v = mm(a_b, g, 1, 0)
            if odd:
                d_key = jnp.concatenate([d_k[:, DR:128], d_k[:, 128 : 128 + DR]], axis=1)
                acc_ref[:, DC + 128 :] += d_k[:, 128:]
            else:
                d_key = d_k[:, :128]
                acc_ref[:, DC : DC + 128] += d_k[:, 128:]
            dkv_ref[:, head * 256 : head * 256 + 128] = d_key.astype(BF16)
            dkv_ref[:, head * 256 + 128 : (head + 1) * 256] = d_v.astype(BF16)
    acc_ref[:, :DC] += mm(dkv_ref[...], w, 1, 1)


def attend(order, lat, rope, bias, alive, w, queries, grads, acc, carried):
    steps = order.shape[0]
    fixed = lambda i, order: (0, 0)
    split = lambda i, order: (0, order[i])
    in_specs = [
        pl.BlockSpec((KEYS, DC), fixed),
        pl.BlockSpec((KEYS, 256), fixed),
        pl.BlockSpec((ROWS, ROWS), fixed),
        pl.BlockSpec((1, ROWS), fixed),
        pl.BlockSpec((1, DC, 1024), lambda i, order: (order[i], 0, 0)),
        pl.BlockSpec((ROWS, 768), split),
        pl.BlockSpec((ROWS, 512), split),
        pl.BlockSpec((KEYS, 768), fixed),
    ]
    args = [order, lat, rope, bias, alive, w, queries, grads, acc]
    aliases = {8: 2}
    if carried is not None:
        in_specs += [pl.BlockSpec(memory_space=pl.ANY)] * 2
        args += list(carried)
        aliases.update({9: 0, 10: 1})
    return pl.pallas_call(
        attend_kernel,
        grid_spec=pltpu.PrefetchScalarGridSpec(
            num_scalar_prefetch=1,
            grid=(steps,),
            in_specs=in_specs,
            out_specs=[
                pl.BlockSpec((ROWS, 512), split),
                pl.BlockSpec((ROWS, 768), split),
                pl.BlockSpec((KEYS, 768), fixed),
            ],
            scratch_shapes=[
                pltpu.VMEM((KEYS, 1024), BF16),
                pltpu.VMEM((KEYS, 1024), BF16),
            ],
        ),
        out_shape=[
            jax.ShapeDtypeStruct((ROWS, 8192), BF16),
            jax.ShapeDtypeStruct((ROWS, 12288), BF16),
            jax.ShapeDtypeStruct((KEYS, 768), F32),
        ],
        input_output_aliases=aliases,
        compiler_params=pltpu.CompilerParams(vmem_limit_bytes=40 * 1024 * 1024),
        cost_estimate=pl.CostEstimate(
            flops=steps * 800_000_000, bytes_accessed=steps * 1_800_000, transcendentals=steps * 131072
        ),
    )(*args)


def body(prompt_latent, resp_latent, queries, d_attended, w_kv, seg_ids, live):
    w = lax.all_gather(w_kv, "prompt", axis=0)
    whole_prompt = lax.all_gather(prompt_latent, "sample", axis=1, tiled=True).reshape(-1, DL)
    rows = jnp.concatenate([whole_prompt, resp_latent.reshape(-1, DL)], axis=0)
    rope = rows[:, DC:]
    blank = jnp.zeros_like(rope)
    rope = jnp.concatenate([rope, blank, blank, rope], axis=1)
    seg = seg_ids[0]
    position = jnp.arange(ROWS, dtype=jnp.int32)
    seen = (
        (seg[:, None] == seg[None, :])
        & (position[:, None] <= position[None, :])
        & (position[:, None] < live[0, 0])
    )
    bias = jnp.where(seen, F32(0.0), F32(-1e30))
    alive = (position < live[0, 0]).astype(F32)[None, :]
    order = jnp.arange(16, dtype=jnp.int32)
    attended, d_queries, acc = attend(
        order, rows[:, :DC], rope, bias, alive, w, queries[0], d_attended[0],
        jnp.zeros((KEYS, 768), F32), None,
    )
    d_rope = acc[:, DC : DC + DR] + acc[:, DC + 128 + DR :]
    term = jnp.concatenate([acc[:, :DC], d_rope], axis=1).astype(BF16)
    pieces = lax.all_to_all(term[:ROWS].reshape(16, -1), "sample", 0, 0)
    d_prompt = jnp.sum(pieces.astype(F32), axis=0).astype(BF16).reshape(1, -1)
    d_resp = term[ROWS:].reshape(1, -1)
    return (attended[None], d_queries[None], d_prompt, d_resp)


def solution(mesh):
    rows = P("prompt", "sample")
    wide = P("prompt", "sample", None)
    return jax.shard_map(
        body,
        mesh=mesh,
        in_specs=(rows, rows, wide, wide, P(None, "prompt"), rows, rows),
        out_specs=(wide, wide, rows, rows),
        check_vma=False,
    )
```

```python
import functools
import jax
import jax.numpy as jnp
from jax import lax
from jax.experimental import pallas as pl
from jax.experimental.pallas import tpu as pltpu
from jax.sharding import PartitionSpec as P

DC = 512
DR = 64
DL = 576
DN = 128
DQ = 192
ROWS = 128
KEYS = 256
HEADS = 4
FLOPS = 4_000_000_000
SCALE = 1.0 / DQ**0.5
LOG2E = 1.4426950408889634
F32 = jnp.float32
BF16 = jnp.bfloat16


def mm(a, b, ca, cb):
    return lax.dot_general(a, b, (((ca,), (cb,)), ((), ())), preferred_element_type=F32)


def attend_kernel(parts, order_ref, lat_ref, rope_ref, bias_ref, alive_ref, q_ref, g_ref, acc_in,
                  *rest):
    w_refs = rest[:parts]
    out_ref, dq_ref, acc_ref, kv_ref, dkv_ref, w_scratch = rest[-6:]

    @pl.when(pl.program_id(0) == 0)
    def _():
        acc_ref[...] = acc_in[...]

    if parts == 1:
        w_ref = w_refs[0].at[0]
    else:
        w_ref = w_scratch
        for index, ref in enumerate(w_refs):
            quarter, late = index // 5 * 4 + min(index % 5, 3), index % 5 == 4
            rows = pl.ds(quarter * 64, 64)
            if index % 5 < 3:
                w_scratch[rows, :] = ref[0]
            else:

                @pl.when((pl.program_id(0) >= pl.num_programs(0) // 2) == late)
                def _():
                    w_scratch[rows, :] = ref[0]

    w = w_ref[...]
    kv_ref[...] = mm(lat_ref[...], w, 1, 0).astype(BF16)
    rope_even = rope_ref[:, :128]
    rope_odd = rope_ref[:, 128:]
    bias = bias_ref[...]
    alive = alive_ref[...]
    low = lax.broadcasted_iota(jnp.int32, (KEYS, 128), 1) < DR
    staged = []
    for pair in range(HEADS // 2):
        for odd in range(2):
            head = pair * 2 + odd
            at = pair * 384 + odd * 128
            q = q_ref[:, at : at + 256]
            g = g_ref[:, head * 128 : (head + 1) * 128]
            key = kv_ref[:, head * 256 : head * 256 + 128]
            value = kv_ref[:, head * 256 + 128 : (head + 1) * 256]
            if odd:
                turned = jnp.concatenate([key[:, DR:], key[:, :DR]], axis=1)
                zero = jnp.zeros_like(turned)
                key_row = jnp.concatenate(
                    [jnp.where(low, zero, turned), jnp.where(low, turned, rope_odd)], axis=1
                )
            else:
                key_row = jnp.concatenate([key, rope_even], axis=1)
            s = mm(key_row, q, 1, 1)
            s = jnp.concatenate([s[:ROWS], s[ROWS:] + bias], axis=0)
            d_a = mm(value, g, 1, 1)
            staged.append((q, g, value, key_row, s, d_a))
    for pair in range(HEADS // 2):
        merged = None
        for odd in range(2):
            head = pair * 2 + odd
            q, g, value, key_row, s, d_a = staged[head]
            top = jnp.max(s, axis=0, keepdims=True)
            e = jnp.exp2((s - top) * (SCALE * LOG2E))
            inv = alive / jnp.sum(e, axis=0, keepdims=True)
            a_b = (e * inv).astype(BF16)
            delta = jnp.sum(e * d_a, axis=0, keepdims=True) * inv
            d_s = ((e * (d_a - delta)) * (inv * SCALE)).astype(BF16)
            out_ref[:, head * 128 : (head + 1) * 128] = mm(a_b, value, 0, 0).astype(BF16)
            d_q = mm(d_s, key_row, 0, 0)
            if odd:
                dq_ref[:, pair * 384 : pair * 384 + 128] = merged[:, :128].astype(BF16)
                dq_ref[:, pair * 384 + 128 : pair * 384 + 256] = (
                    merged[:, 128:] + d_q[:, :128]
                ).astype(BF16)
                dq_ref[:, pair * 384 + 256 : pair * 384 + 384] = d_q[:, 128:].astype(BF16)
            else:
                merged = d_q
            d_k = mm(d_s, q, 1, 0)
            d_v = mm(a_b, g, 1, 0)
            if odd:
                d_key = jnp.concatenate([d_k[:, DR:128], d_k[:, 128 : 128 + DR]], axis=1)
                acc_ref[:, DC + 128 :] += d_k[:, 128:]
            else:
                d_key = d_k[:, :128]
                acc_ref[:, DC : DC + 128] += d_k[:, 128:]
            dkv_ref[:, head * 256 : head * 256 + 128] = d_key.astype(BF16)
            dkv_ref[:, head * 256 + 128 : (head + 1) * 256] = d_v.astype(BF16)
    acc_ref[:, :DC] += mm(dkv_ref[...], w, 1, 1)


def attend(order, lat, rope, bias, alive, weights, queries, grads, acc, carried):
    steps = order.shape[0]
    fixed = lambda i, order: (0, 0)
    split = lambda i, order: (0, order[i])
    in_specs = [
        pl.BlockSpec((KEYS, DC), fixed),
        pl.BlockSpec((KEYS, 256), fixed),
        pl.BlockSpec((ROWS, ROWS), fixed),
        pl.BlockSpec((1, ROWS), fixed),
        pl.BlockSpec((ROWS, 768), split),
        pl.BlockSpec((ROWS, 512), split),
        pl.BlockSpec((KEYS, 768), fixed),
    ]
    args = [order, lat, rope, bias, alive, queries, grads, acc]
    half = steps // 2
    for index, w in enumerate(weights):
        if index % 5 < 3:
            place = lambda i, order: (i, 0, 0)
        elif index % 5 == 3:
            place = lambda i, order: (jnp.minimum(i, half - 1), 0, 0)
        else:
            place = lambda i, order: (jnp.maximum(i - half, 0), 0, 0)
        in_specs.append(pl.BlockSpec((1,) + w.shape[1:], place))
        args.append(w)
    aliases = {7: 2}
    if carried is not None:
        aliases.update({len(args): 0, len(args) + 1: 1})
        in_specs += [pl.BlockSpec(memory_space=pl.ANY)] * 2
        args += list(carried)
    return pl.pallas_call(
        functools.partial(attend_kernel, len(weights)),
        grid_spec=pltpu.PrefetchScalarGridSpec(
            num_scalar_prefetch=1,
            grid=(steps,),
            in_specs=in_specs,
            out_specs=[
                pl.BlockSpec((ROWS, 512), split),
                pl.BlockSpec((ROWS, 768), split),
                pl.BlockSpec((KEYS, 768), fixed),
            ],
            scratch_shapes=[
                pltpu.VMEM((KEYS, 1024), BF16),
                pltpu.VMEM((KEYS, 1024), BF16),
                pltpu.VMEM((DC, 1024), BF16),
            ],
        ),
        out_shape=[
            jax.ShapeDtypeStruct((ROWS, 8192), BF16),
            jax.ShapeDtypeStruct((ROWS, 12288), BF16),
            jax.ShapeDtypeStruct((KEYS, 768), F32),
        ],
        input_output_aliases=aliases,
        compiler_params=pltpu.CompilerParams(vmem_limit_bytes=40 * 1024 * 1024),
        cost_estimate=pl.CostEstimate(
            flops=steps * FLOPS, bytes_accessed=steps * 1_800_000, transcendentals=0
        ),
    )(*args)


def at(x, y, z, core):
    return ((z % 8) * 2 + core) * 16 + (x % 4) * 4 + y % 4


CHIPS = [(x, y, z) for x in range(4) for y in range(4) for z in range(8)]
SWAP = [(at(x, y, z, c), at(x, y, z, 1 - c)) for x, y, z in CHIPS for c in range(2)]


def along_z(step):
    return [(at(x, y, z, c), at(x, y, z + step, c)) for x, y, z in CHIPS for c in range(2)]


def along_plane(step):
    return [(at(x, y, z, 0), at(x + step, y, z, 0)) for x, y, z in CHIPS] + [
        (at(x, y, z, 1), at(x, y + step, z, 1)) for x, y, z in CHIPS
    ]


def send(a, pairs):
    return lax.ppermute(a, ("prompt", "sample"), pairs)


def places():
    prompt, sample = lax.axis_index("prompt"), lax.axis_index("sample")
    z, core = prompt // 2, prompt % 2
    x, y = sample // 4, sample % 4
    mine = jnp.where(core == 0, x, y)
    other = jnp.where(core == 0, y, x)
    return z, core, mine, other


def z_slices(w):
    z, core, mine, other = places()
    parts = w.reshape(8, -1, w.shape[1])
    keep = lax.dynamic_index_in_dim(parts, core * 4 + mine, 0, keepdims=True)
    give = lax.dynamic_index_in_dim(parts, (1 - core) * 4 + other, 0, keepdims=True)
    got = send(give, SWAP)
    here = jnp.where(core == 0, jnp.concatenate([keep, got]), jnp.concatenate([got, keep]))
    down, up = [here], [here]
    for _ in range(3):
        down.append(send(down[-1], along_z(1)))
        up.append(send(up[-1], along_z(-1)))
    far = jnp.concatenate([send(down[3][:1], along_z(1)), send(up[3][1:], along_z(-1))])
    return down, up, far


def plane_gather(group):
    half = group.shape[0] // 2
    left = send(group, along_plane(1))
    right = send(group, along_plane(-1))
    early = send(left[:half], along_plane(1))
    late = send(right[half:], along_plane(-1))
    pieces = [group, left, right, early, late]
    return pieces + [send(piece, SWAP) for piece in pieces]


def row_order():
    z, core, mine, other = places()
    turn = jnp.array([0, 3, 1, 2], jnp.int32)
    return jnp.concatenate([core * 4 + (mine + turn) % 4, (1 - core) * 4 + (other + turn) % 4])


def body(prompt_latent, resp_latent, queries, d_attended, w_kv, seg_ids, live):
    z, core, mine, other = places()
    prompt = 2 * z + core
    down, up, far = z_slices(w_kv)
    pair = jnp.stack([w_kv, send(w_kv, SWAP)])
    whole_prompt = lax.all_to_all(
        jnp.tile(prompt_latent.reshape(-1, DL), (16, 1)), "sample", 0, 0, tiled=True
    )
    rows = jnp.concatenate([whole_prompt, resp_latent.reshape(-1, DL)], axis=0)
    rope = rows[:, DC:]
    blank = jnp.zeros_like(rope)
    rope = jnp.concatenate([rope, blank, blank, rope], axis=1)
    seg = seg_ids[0]
    position = jnp.arange(ROWS, dtype=jnp.int32)
    seen = (
        (seg[:, None] == seg[None, :])
        & (position[:, None] <= position[None, :])
        & (position[:, None] < live[0, 0])
    )
    bias = jnp.where(seen, F32(0.0), F32(-1e30))
    alive = (position < live[0, 0]).astype(F32)[None, :]
    lat = rows[:, :DC]
    index = jnp.arange(DC, dtype=jnp.int32)
    source = jnp.repeat(row_order() * 64, 64) + index % 64
    turn = (index[:, None] == source[None, :]).astype(BF16)
    lat_turned = jnp.dot(lat, turn, preferred_element_type=F32).astype(BF16)

    attended, d_queries, acc = attend(
        jnp.stack([prompt, prompt ^ 1]), lat, rope, bias, alive, [pair], queries[0], d_attended[0],
        jnp.zeros((KEYS, 768), F32), None,
    )
    first = acc
    acc = jnp.zeros((KEYS, 768), F32)
    for group, steps in enumerate(((-1, 1, -2, 2), (-3, 3, 4))):
        pieces = []
        for step in steps:
            pieces.append(far if step == 4 else (up[step] if step > 0 else down[-step]))
        weights = plane_gather(jnp.concatenate(pieces))
        order = jnp.concatenate([2 * ((z + step) % 8) + jnp.arange(2) for step in steps])
        attended, d_queries, acc = attend(
            order.astype(jnp.int32), lat_turned, rope, bias, alive,
            weights, queries[0], d_attended[0], acc, (attended, d_queries),
        )
    latent = first[:, :DC] + jnp.dot(
        acc[:, :DC], turn.T.astype(F32), precision=lax.Precision.HIGHEST, preferred_element_type=F32
    )
    both = first[:, DC:] + acc[:, DC:]
    term = jnp.concatenate([latent, both[:, :DR] + both[:, 128 + DR :]], axis=1).astype(BF16)
    pieces = lax.all_to_all(term[:ROWS], "sample", 0, 0, tiled=True).reshape(16, -1, DL)
    d_prompt = jnp.sum(pieces.astype(F32), axis=0).astype(BF16).reshape(1, -1)
    d_resp = term[ROWS:].reshape(1, -1)
    return (attended[None], d_queries[None], d_prompt, d_resp)


def solution(mesh):
    rows = P("prompt", "sample")
    wide = P("prompt", "sample", None)
    return jax.shard_map(
        body,
        mesh=mesh,
        in_specs=(rows, rows, wide, wide, P(None, "prompt"), rows, rows),
        out_specs=(wide, wide, rows, rows),
        check_vma=False,
    )
```

```python
import functools
import jax
import jax.numpy as jnp
from jax import lax
from jax.experimental import pallas as pl
from jax.experimental.pallas import tpu as pltpu
from jax.sharding import PartitionSpec as P

DC = 512
DR = 64
DL = 576
DN = 128
DQ = 192
ROWS = 128
KEYS = 256
HEADS = 4
VMEM = 60
FLOPS = 4_000_000_000
SCALE = 1.0 / DQ**0.5
LOG2E = 1.4426950408889634
F32 = jnp.float32
BF16 = jnp.bfloat16


def mm(a, b, ca, cb):
    return lax.dot_general(a, b, (((ca,), (cb,)), ((), ())), preferred_element_type=F32)


def attend_kernel(layout, more, last, order_ref, rows_hbm, mask_hbm, q_hbm, g_hbm, *rest):
    w_hbm = rest[more : more + 1 + max(entry[0] for entry in layout)]
    outs = rest[:-11][-4 if last else -3 :]
    out_ref, dq_ref = outs[:2]
    rows_ref, mask_ref, q_all, g_all, w_all, before_ref, acc_ref, kv_ref, dkv_ref = rest[-11:-2]
    arrived, loaded = rest[-2:]
    step, steps = pl.program_id(0), w_all.shape[0]

    def piece(index):
        source, shard, slot, row = layout[index]
        first = 0 if row is None else pl.multiple_of(order_ref[steps + row], 128)
        ref = w_hbm[source].at[shard]
        return pltpu.make_async_copy(
            ref, w_all.at[slot, pl.ds(first, ref.shape[0])], arrived.at[slot]
        )

    def block(ref, all_ref, slot, number, sem):
        width = all_ref.shape[2]
        columns = pl.ds(pl.multiple_of(order_ref[number] * width, width), width)
        return pltpu.make_async_copy(ref.at[:, columns], all_ref.at[slot], loaded.at[sem])

    rows_copy = pltpu.make_async_copy(rows_hbm, rows_ref, loaded.at[2 * steps])
    mask_copy = pltpu.make_async_copy(mask_hbm, mask_ref, loaded.at[2 * steps + 1])
    if more:
        before_copy = pltpu.make_async_copy(rest[0], before_ref, loaded.at[2 * steps + 2])

    def ask(slot):
        for index, entry in enumerate(layout):
            if entry[2] == slot:
                piece(index).start()
        block(q_hbm, q_all, slot, slot, slot).start()
        block(g_hbm, g_all, slot, slot, steps + slot).start()

    @pl.when(step == 0)
    def _():
        rows_copy.start()
        ask(0)
        mask_copy.start()
        ask(1)
        acc_ref[...] = jnp.zeros_like(acc_ref)
        rows_copy.wait()
        mask_copy.wait()

    @pl.when(step == 1)
    def _():
        for slot in range(2, steps):
            ask(slot)
        if more:
            before_copy.start()

    pltpu.make_async_copy(w_all.at[step], w_all.at[step], arrived.at[step]).wait()
    pltpu.make_async_copy(q_all.at[step], q_all.at[step], loaded.at[step]).wait()
    pltpu.make_async_copy(g_all.at[step], g_all.at[step], loaded.at[steps + step]).wait()
    q_ref, g_ref = q_all.at[step], g_all.at[step]
    w = w_all[step]
    kv_ref[...] = mm(rows_ref[:, :DC], w, 1, 0).astype(BF16)
    rope_even = rows_ref[:, DC : DC + 128]
    rope_odd = rows_ref[:, DC + 128 :]
    bias = mask_ref[:ROWS, :]
    alive = mask_ref[ROWS : ROWS + 1, :]
    low = lax.broadcasted_iota(jnp.int32, (KEYS, 128), 1) < DR
    staged = []
    for pair in range(HEADS // 2):
        for odd in range(2):
            head = pair * 2 + odd
            at = pair * 384 + odd * 128
            q = q_ref[:, at : at + 256]
            g = g_ref[:, head * 128 : (head + 1) * 128]
            key = kv_ref[:, head * 256 : head * 256 + 128]
            value = kv_ref[:, head * 256 + 128 : (head + 1) * 256]
            if odd:
                turned = jnp.concatenate([key[:, DR:], key[:, :DR]], axis=1)
                zero = jnp.zeros_like(turned)
                key_row = jnp.concatenate(
                    [jnp.where(low, zero, turned), jnp.where(low, turned, rope_odd)], axis=1
                )
            else:
                key_row = jnp.concatenate([key, rope_even], axis=1)
            s = mm(key_row, q, 1, 1)
            s = jnp.concatenate([s[:ROWS], s[ROWS:] + bias], axis=0)
            d_a = mm(value, g, 1, 1)
            staged.append((q, g, value, key_row, s, d_a))
    for pair in range(HEADS // 2):
        merged = None
        for odd in range(2):
            head = pair * 2 + odd
            q, g, value, key_row, s, d_a = staged[head]
            top = jnp.max(s, axis=0, keepdims=True)
            e = jnp.exp2((s - top) * (SCALE * LOG2E))
            inv = alive / jnp.sum(e, axis=0, keepdims=True)
            a_b = (e * inv).astype(BF16)
            delta = jnp.sum(e * d_a, axis=0, keepdims=True) * inv
            d_s = ((e * (d_a - delta)) * (inv * SCALE)).astype(BF16)
            out_ref[:, head * 128 : (head + 1) * 128] = mm(a_b, value, 0, 0).astype(BF16)
            d_q = mm(d_s, key_row, 0, 0)
            if odd:
                dq_ref[:, pair * 384 : pair * 384 + 128] = merged[:, :128].astype(BF16)
                dq_ref[:, pair * 384 + 128 : pair * 384 + 256] = (
                    merged[:, 128:] + d_q[:, :128]
                ).astype(BF16)
                dq_ref[:, pair * 384 + 256 : pair * 384 + 384] = d_q[:, 128:].astype(BF16)
            else:
                merged = d_q
            d_k = mm(d_s, q, 1, 0)
            d_v = mm(a_b, g, 1, 0)
            if odd:
                d_key = jnp.concatenate([d_k[:, DR:128], d_k[:, 128 : 128 + DR]], axis=1)
                acc_ref[:, DC + 128 :] += d_k[:, 128:]
            else:
                d_key = d_k[:, :128]
                acc_ref[:, DC : DC + 128] += d_k[:, 128:]
            dkv_ref[:, head * 256 : head * 256 + 128] = d_key.astype(BF16)
            dkv_ref[:, head * 256 + 128 : (head + 1) * 256] = d_v.astype(BF16)
    acc_ref[:, :DC] += mm(dkv_ref[...], w, 1, 1)


    @pl.when(step == steps - 1)
    def _():
        total = acc_ref[...]
        if more:
            before_copy.wait()
            total += before_ref[...]
        if last:
            rope_sum = total[:, DC : DC + DR] + total[:, DC + 128 + DR :]
            for ref, rows in zip(outs[2:], (slice(0, ROWS), slice(ROWS, KEYS))):
                ref[:, :DC] = total[rows, :DC].astype(BF16)
                ref[:, DC:] = rope_sum[rows].astype(BF16)
        else:
            outs[2][...] = total


def attend(order, rows, mask, weights, layout, queries, grads, before=(), last=False):
    steps = 1 + max(entry[2] for entry in layout)
    split = lambda i, order: (0, order[i])
    args = [order, rows, mask, queries, grads]
    args += list(before[2:]) + list(weights) + list(before[:2])
    aliases = {len(args) - 2: 0, len(args) - 1: 1} if before else {}
    results = [jax.ShapeDtypeStruct((KEYS, 768), F32)]
    if last:
        results = [jax.ShapeDtypeStruct((ROWS, DL), BF16)] * 2
    return pl.pallas_call(
        functools.partial(attend_kernel, layout, int(bool(before)), last),
        grid_spec=pltpu.PrefetchScalarGridSpec(
            num_scalar_prefetch=1,
            grid=(steps,),
            in_specs=[pl.BlockSpec(memory_space=pl.ANY)] * (len(args) - 1),
            out_specs=[
                pl.BlockSpec((ROWS, 512), split),
                pl.BlockSpec((ROWS, 768), split),
            ]
            + [pl.BlockSpec(result.shape, lambda i, order: (0, 0)) for result in results],
            scratch_shapes=[
                pltpu.VMEM((KEYS, 768), BF16),
                pltpu.VMEM((ROWS + 8, 128), F32),
                pltpu.VMEM((steps, ROWS, 768), BF16),
                pltpu.VMEM((steps, ROWS, 512), BF16),
                pltpu.VMEM((steps, DC, 1024), BF16),
                pltpu.VMEM((KEYS, 768), F32),
                pltpu.VMEM((KEYS, 768), F32),
                pltpu.VMEM((KEYS, 1024), BF16),
                pltpu.VMEM((KEYS, 1024), BF16),
                pltpu.SemaphoreType.DMA((steps,)),
                pltpu.SemaphoreType.DMA((2 * steps + 3,)),
            ],
        ),
        out_shape=[
            jax.ShapeDtypeStruct((ROWS, 8192), BF16),
            jax.ShapeDtypeStruct((ROWS, 12288), BF16),
        ]
        + results,
        input_output_aliases=aliases,
        compiler_params=pltpu.CompilerParams(vmem_limit_bytes=VMEM * 1024 * 1024),
        cost_estimate=pl.CostEstimate(
            flops=steps * FLOPS, bytes_accessed=steps * 1_800_000, transcendentals=0
        ),
    )(*args)


def at(x, y, z, core):
    return ((z % 8) * 2 + core) * 16 + (x % 4) * 4 + y % 4


CHIPS = [(x, y, z) for x in range(4) for y in range(4) for z in range(8)]
SWAP = [(at(x, y, z, c), at(x, y, z, 1 - c)) for x, y, z in CHIPS for c in range(2)]


RING = [(at(x, y, z, 0), at(x, y, z + 1, 0)) for x, y, z in CHIPS] + [
    (at(x, y, z, 1), at(x, y, z - 1, 1)) for x, y, z in CHIPS
]
PLANE = [(at(x, y, z, 0), at(x + 1, y, z, 0)) for x, y, z in CHIPS] + [
    (at(x, y, z, 1), at(x, y + 1, z, 1)) for x, y, z in CHIPS
]


def send(a, pairs):
    return lax.ppermute(a, ("prompt", "sample"), pairs)


def places():
    prompt, sample = lax.axis_index("prompt"), lax.axis_index("sample")
    z, core = prompt // 2, prompt % 2
    x, y = sample // 4, sample % 4
    mine = jnp.where(core == 0, x, y)
    other = jnp.where(core == 0, y, x)
    return z, core, mine, other


def after(a, *done):
    return lax.optimization_barrier((a,) + done)[0]


def around(piece):
    local = [piece, send(piece, PLANE)]
    return local + [send(part, SWAP) for part in local]


def layout_of(source, slot, shards):
    return tuple(
        (source + 2 * way + part, shard, slot + way * shards + shard, 2 * way + part)
        for way in (0, 1)
        for shard in range(shards)
        for part in (0, 1)
    )


def body(prompt_latent, resp_latent, queries, d_attended, w_kv, seg_ids, live):
    z, core, mine, other = places()
    prompt = 2 * z + core
    half, other_half = mine % 2 * 256, other % 2 * 256
    pair = [w_kv, send(w_kv, SWAP)]
    here = jnp.stack([lax.dynamic_slice_in_dim(w, half, 256, 0) for w in pair])
    ring = send(here, RING)
    pair = [w[None] for w in pair]
    whole_prompt = lax.all_to_all(
        jnp.tile(after(prompt_latent, here).reshape(-1, DL), (16, 1)), "sample", 0, 0, tiled=True
    )
    rows = jnp.concatenate([whole_prompt, resp_latent.reshape(-1, DL)], axis=0)
    blank = jnp.zeros((KEYS, 128), BF16)
    rows = jnp.concatenate([rows, blank, rows[:, DC:]], axis=1)
    seg = seg_ids[0]
    position = jnp.arange(ROWS, dtype=jnp.int32)
    seen = (
        (seg[:, None] == seg[None, :])
        & (position[:, None] <= position[None, :])
        & (position[:, None] < live[0, 0])
    )
    bias = jnp.where(seen, F32(0.0), F32(-1e30))
    alive = (position < live[0, 0]).astype(F32)[None, :]
    mask = jnp.concatenate([bias, jnp.broadcast_to(alive, (8, ROWS))], axis=0)
    ring, rows, mask = lax.optimization_barrier((ring, rows, mask))
    tensors = (queries[0], d_attended[0])
    starts = jnp.stack([half, 256 - half, other_half, 256 - other_half])
    way = 2 * core - 1

    def order(*steps):
        numbers = []
        for step in steps:
            if step in (0, 4):
                numbers += [2 * ((z + step) % 8) + core, 2 * ((z + step) % 8) + 1 - core]
            else:
                near, far = 2 * ((z + way * step) % 8), 2 * ((z - way * step) % 8)
                numbers += [near + core, near + 1 - core, far + 1 - core, far + core]
        return jnp.concatenate([jnp.stack(numbers), starts]).astype(jnp.int32)

    pair_layout = ((0, 0, 0, None), (1, 0, 1, None))
    results = attend(
        order(0, 1), rows, mask, pair + around(ring), pair_layout + layout_of(2, 2, 2), *tensors
    )
    ring = send(ring, RING)
    second = around(ring)
    ring, before = lax.optimization_barrier((send(ring, RING), results[2]))
    attended, d_queries, prompt_term, resp_term = attend(
        order(2, 3, 4), rows, mask, second + around(ring) + around(send(ring[:1], RING)),
        layout_of(0, 0, 2) + layout_of(4, 4, 2) + layout_of(8, 8, 1),
        *tensors, [*results[:2], before], last=True,
    )
    pieces = lax.all_to_all(prompt_term, "sample", 0, 0, tiled=True).reshape(16, -1, DL)
    d_prompt = jnp.sum(pieces.astype(F32), axis=0).astype(BF16).reshape(1, -1)
    d_resp = resp_term.reshape(1, -1)
    return (attended[None], d_queries[None], d_prompt, d_resp)


def solution(mesh):
    rows = P("prompt", "sample")
    wide = P("prompt", "sample", None)
    return jax.shard_map(
        body,
        mesh=mesh,
        in_specs=(rows, rows, wide, wide, P(None, "prompt"), rows, rows),
        out_specs=(wide, wide, rows, rows),
        check_vma=False,
    )
```

```python
import functools
import jax
import jax.numpy as jnp
from jax import lax
from jax.experimental import pallas as pl
from jax.experimental.pallas import tpu as pltpu
from jax.sharding import PartitionSpec as P

DC = 512
DR = 64
DL = 576
DN = 128
DQ = 192
ROWS = 128
KEYS = 256
HEADS = 4
VMEM = 60
FLOPS = 4_000_000_000
SCALE = 1.0 / DQ**0.5
LOG2E = 1.4426950408889634
F32 = jnp.float32
BF16 = jnp.bfloat16


def mm(a, b, ca, cb):
    return lax.dot_general(a, b, (((ca,), (cb,)), ((), ())), preferred_element_type=F32)


def attend_kernel(layout, more, last, order_ref, rows_hbm, mask_hbm, q_hbm, g_hbm, *rest):
    w_hbm = rest[more : more + 1 + max(entry[0] for entry in layout)]
    outs = rest[:-11][-4 if last else -3 :]
    out_ref, dq_ref = outs[:2]
    rows_ref, mask_ref, q_all, g_all, w_all, before_ref, acc_ref, kv_ref, dkv_ref = rest[-11:-2]
    arrived, loaded = rest[-2:]
    step, steps = pl.program_id(0), w_all.shape[0]

    def piece(index):
        source, shard, slot, row = layout[index]
        first = 0 if row is None else pl.multiple_of(order_ref[steps + row], 128)
        ref = w_hbm[source].at[shard]
        return pltpu.make_async_copy(
            ref, w_all.at[slot, pl.ds(first, ref.shape[0])], arrived.at[slot]
        )

    def block(ref, all_ref, slot, number, sem):
        width = all_ref.shape[2]
        columns = pl.ds(pl.multiple_of(order_ref[number] * width, width), width)
        return pltpu.make_async_copy(ref.at[:, columns], all_ref.at[slot], loaded.at[sem])

    rows_copy = pltpu.make_async_copy(rows_hbm, rows_ref, loaded.at[2 * steps])
    mask_copy = pltpu.make_async_copy(mask_hbm, mask_ref, loaded.at[2 * steps + 1])
    if more:
        before_copy = pltpu.make_async_copy(rest[0], before_ref, loaded.at[2 * steps + 2])

    def ask(slot):
        for index, entry in enumerate(layout):
            if entry[2] == slot:
                piece(index).start()
        block(q_hbm, q_all, slot, slot, slot).start()
        block(g_hbm, g_all, slot, slot, steps + slot).start()

    @pl.when(step == 0)
    def _():
        rows_copy.start()
        ask(0)
        mask_copy.start()
        acc_ref[...] = jnp.zeros_like(acc_ref)
        rows_copy.wait()
        mask_copy.wait()

    pltpu.make_async_copy(w_all.at[step], w_all.at[step], arrived.at[step]).wait()
    pltpu.make_async_copy(q_all.at[step], q_all.at[step], loaded.at[step]).wait()
    pltpu.make_async_copy(g_all.at[step], g_all.at[step], loaded.at[steps + step]).wait()

    @pl.when(step == 0)
    def _():
        for slot in range(1, steps):
            ask(slot)
        if more:
            before_copy.start()

    q_ref, g_ref = q_all.at[step], g_all.at[step]
    w = w_all[step]
    kv_ref[...] = mm(rows_ref[:, :DC], w, 1, 0).astype(BF16)
    rope_even = rows_ref[:, DC : DC + 128]
    rope_odd = rows_ref[:, DC + 128 :]
    bias = mask_ref[:ROWS, :]
    alive = mask_ref[ROWS : ROWS + 1, :]
    low = lax.broadcasted_iota(jnp.int32, (KEYS, 128), 1) < DR
    staged = []
    for pair in range(HEADS // 2):
        for odd in range(2):
            head = pair * 2 + odd
            at = pair * 384 + odd * 128
            q = q_ref[:, at : at + 256]
            g = g_ref[:, head * 128 : (head + 1) * 128]
            key = kv_ref[:, head * 256 : head * 256 + 128]
            value = kv_ref[:, head * 256 + 128 : (head + 1) * 256]
            if odd:
                turned = jnp.concatenate([key[:, DR:], key[:, :DR]], axis=1)
                zero = jnp.zeros_like(turned)
                key_row = jnp.concatenate(
                    [jnp.where(low, zero, turned), jnp.where(low, turned, rope_odd)], axis=1
                )
            else:
                key_row = jnp.concatenate([key, rope_even], axis=1)
            s = mm(key_row, q, 1, 1)
            s = jnp.concatenate([s[:ROWS], s[ROWS:] + bias], axis=0)
            d_a = mm(value, g, 1, 1)
            staged.append((q, g, value, key_row, s, d_a))
    for pair in range(HEADS // 2):
        merged = None
        for odd in range(2):
            head = pair * 2 + odd
            q, g, value, key_row, s, d_a = staged[head]
            top = jnp.max(s, axis=0, keepdims=True)
            e = jnp.exp2((s - top) * (SCALE * LOG2E))
            inv = alive / jnp.sum(e, axis=0, keepdims=True)
            a_b = (e * inv).astype(BF16)
            delta = jnp.sum(e * d_a, axis=0, keepdims=True) * inv
            d_s = ((e * (d_a - delta)) * (inv * SCALE)).astype(BF16)
            out_ref[:, head * 128 : (head + 1) * 128] = mm(a_b, value, 0, 0).astype(BF16)
            d_q = mm(d_s, key_row, 0, 0)
            if odd:
                dq_ref[:, pair * 384 : pair * 384 + 128] = merged[:, :128].astype(BF16)
                dq_ref[:, pair * 384 + 128 : pair * 384 + 256] = (
                    merged[:, 128:] + d_q[:, :128]
                ).astype(BF16)
                dq_ref[:, pair * 384 + 256 : pair * 384 + 384] = d_q[:, 128:].astype(BF16)
            else:
                merged = d_q
            d_k = mm(d_s, q, 1, 0)
            d_v = mm(a_b, g, 1, 0)
            if odd:
                d_key = jnp.concatenate([d_k[:, DR:128], d_k[:, 128 : 128 + DR]], axis=1)
                acc_ref[:, DC + 128 :] += d_k[:, 128:]
            else:
                d_key = d_k[:, :128]
                acc_ref[:, DC : DC + 128] += d_k[:, 128:]
            dkv_ref[:, head * 256 : head * 256 + 128] = d_key.astype(BF16)
            dkv_ref[:, head * 256 + 128 : (head + 1) * 256] = d_v.astype(BF16)
    acc_ref[:, :DC] += mm(dkv_ref[...], w, 1, 1)


    @pl.when(step == steps - 1)
    def _():
        total = acc_ref[...]
        if more:
            before_copy.wait()
            total += before_ref[...]
        if last:
            rope_sum = total[:, DC : DC + DR] + total[:, DC + 128 + DR :]
            for ref, rows in zip(outs[2:], (slice(0, ROWS), slice(ROWS, KEYS))):
                ref[:, :DC] = total[rows, :DC].astype(BF16)
                ref[:, DC:] = rope_sum[rows].astype(BF16)
        else:
            outs[2][...] = total


def attend(order, rows, mask, weights, layout, queries, grads, before=(), last=False):
    steps = 1 + max(entry[2] for entry in layout)
    split = lambda i, order: (0, order[i])
    args = [order, rows, mask, queries, grads]
    args += list(before[2:]) + list(weights) + list(before[:2])
    aliases = {len(args) - 2: 0, len(args) - 1: 1} if before else {}
    results = [jax.ShapeDtypeStruct((KEYS, 768), F32)]
    if last:
        results = [jax.ShapeDtypeStruct((ROWS, DL), BF16)] * 2
    return pl.pallas_call(
        functools.partial(attend_kernel, layout, int(bool(before)), last),
        grid_spec=pltpu.PrefetchScalarGridSpec(
            num_scalar_prefetch=1,
            grid=(steps,),
            in_specs=[pl.BlockSpec(memory_space=pl.ANY)] * (len(args) - 1),
            out_specs=[
                pl.BlockSpec((ROWS, 512), split),
                pl.BlockSpec((ROWS, 768), split),
            ]
            + [pl.BlockSpec(result.shape, lambda i, order: (0, 0)) for result in results],
            scratch_shapes=[
                pltpu.VMEM((KEYS, 768), BF16),
                pltpu.VMEM((ROWS + 8, 128), F32),
                pltpu.VMEM((steps, ROWS, 768), BF16),
                pltpu.VMEM((steps, ROWS, 512), BF16),
                pltpu.VMEM((steps, DC, 1024), BF16),
                pltpu.VMEM((KEYS, 768), F32),
                pltpu.VMEM((KEYS, 768), F32),
                pltpu.VMEM((KEYS, 1024), BF16),
                pltpu.VMEM((KEYS, 1024), BF16),
                pltpu.SemaphoreType.DMA((steps,)),
                pltpu.SemaphoreType.DMA((2 * steps + 3,)),
            ],
        ),
        out_shape=[
            jax.ShapeDtypeStruct((ROWS, 8192), BF16),
            jax.ShapeDtypeStruct((ROWS, 12288), BF16),
        ]
        + results,
        input_output_aliases=aliases,
        compiler_params=pltpu.CompilerParams(vmem_limit_bytes=VMEM * 1024 * 1024),
        cost_estimate=pl.CostEstimate(
            flops=steps * FLOPS, bytes_accessed=steps * 1_800_000, transcendentals=0
        ),
    )(*args)


def at(x, y, z, core):
    return ((z % 8) * 2 + core) * 16 + (x % 4) * 4 + y % 4


CHIPS = [(x, y, z) for x in range(4) for y in range(4) for z in range(8)]
SWAP = [(at(x, y, z, c), at(x, y, z, 1 - c)) for x, y, z in CHIPS for c in range(2)]


RING = [(at(x, y, z, 0), at(x, y, z + 1, 0)) for x, y, z in CHIPS] + [
    (at(x, y, z, 1), at(x, y, z - 1, 1)) for x, y, z in CHIPS
]
PLANE = [(at(x, y, z, 0), at(x + 1, y, z, 0)) for x, y, z in CHIPS] + [
    (at(x, y, z, 1), at(x, y + 1, z, 1)) for x, y, z in CHIPS
]


def send(a, pairs):
    return lax.ppermute(a, ("prompt", "sample"), pairs)


def places():
    prompt, sample = lax.axis_index("prompt"), lax.axis_index("sample")
    z, core = prompt // 2, prompt % 2
    x, y = sample // 4, sample % 4
    mine = jnp.where(core == 0, x, y)
    other = jnp.where(core == 0, y, x)
    return z, core, mine, other


def after(a, *done):
    return lax.optimization_barrier((a,) + done)[0]


def with_other_core(piece, rest):
    return [piece, rest, send(piece, SWAP), send(rest, SWAP)]


def layout_of(source, slot, shards):
    return tuple(
        (source + 2 * way + part, shard, slot + way * shards + shard, 2 * way + part)
        for way in (0, 1)
        for shard in range(shards)
        for part in (0, 1)
    )


def body(prompt_latent, resp_latent, queries, d_attended, w_kv, seg_ids, live):
    z, core, mine, other = places()
    prompt = 2 * z + core
    half, other_half = mine % 2 * 256, other % 2 * 256
    pair = [w_kv, send(w_kv, SWAP)]
    here = jnp.stack([lax.dynamic_slice_in_dim(w, half, 256, 0) for w in pair])
    ring = send(here, RING)
    pair = [w[None] for w in pair]
    whole_prompt = lax.all_to_all(
        jnp.tile(after(prompt_latent, here).reshape(-1, DL), (16, 1)), "sample", 0, 0, tiled=True
    )
    rows = jnp.concatenate([whole_prompt, resp_latent.reshape(-1, DL)], axis=0)
    blank = jnp.zeros((KEYS, 128), BF16)
    rows = jnp.concatenate([rows, blank, rows[:, DC:]], axis=1)
    seg = seg_ids[0]
    position = jnp.arange(ROWS, dtype=jnp.int32)
    seen = (
        (seg[:, None] == seg[None, :])
        & (position[:, None] <= position[None, :])
        & (position[:, None] < live[0, 0])
    )
    bias = jnp.where(seen, F32(0.0), F32(-1e30))
    alive = (position < live[0, 0]).astype(F32)[None, :]
    mask = jnp.concatenate([bias, jnp.broadcast_to(alive, (8, ROWS))], axis=0)
    ring, rows, mask = lax.optimization_barrier((ring, rows, mask))
    tensors = (queries[0], d_attended[0])
    starts = jnp.stack([half, 256 - half, other_half, 256 - other_half])
    way = 2 * core - 1

    def order(*steps):
        numbers = []
        for step in steps:
            if step in (0, 4):
                numbers += [2 * ((z + step) % 8) + core, 2 * ((z + step) % 8) + 1 - core]
            else:
                near, far = 2 * ((z + way * step) % 8), 2 * ((z - way * step) % 8)
                numbers += [near + core, near + 1 - core, far + 1 - core, far + core]
        return jnp.concatenate([jnp.stack(numbers), starts]).astype(jnp.int32)

    pair_layout = ((0, 0, 0, None), (1, 0, 1, None))
    results = attend(order(0), rows, mask, pair, pair_layout, *tensors)
    rest1, ring2, before = lax.optimization_barrier(
        (send(ring, PLANE), send(ring, RING), results[2])
    )
    results = attend(
        order(1), rows, mask, with_other_core(ring, rest1), layout_of(0, 0, 2),
        *tensors, [*results[:2], before],
    )
    second = with_other_core(ring2, send(ring2, PLANE))
    ring3, before = lax.optimization_barrier((send(ring2, RING), results[2]))
    ring4 = send(ring3[:1], RING)
    rest3, rest4 = lax.optimization_barrier((send(ring3, PLANE), send(ring4, PLANE)))
    third = with_other_core(ring3, rest3)
    fourth = with_other_core(ring4, rest4)
    attended, d_queries, prompt_term, resp_term = attend(
        order(2, 3, 4), rows, mask, second + third + fourth,
        layout_of(0, 0, 2) + layout_of(4, 4, 2) + layout_of(8, 8, 1),
        *tensors, [*results[:2], before], last=True,
    )
    pieces = lax.all_to_all(prompt_term, "sample", 0, 0, tiled=True).reshape(16, -1, DL)
    d_prompt = jnp.sum(pieces.astype(F32), axis=0).astype(BF16).reshape(1, -1)
    d_resp = resp_term.reshape(1, -1)
    return (attended[None], d_queries[None], d_prompt, d_resp)


def solution(mesh):
    rows = P("prompt", "sample")
    wide = P("prompt", "sample", None)
    return jax.shard_map(
        body,
        mesh=mesh,
        in_specs=(rows, rows, wide, wide, P(None, "prompt"), rows, rows),
        out_specs=(wide, wide, rows, rows),
        check_vma=False,
    )
```

```python
import functools
import jax
import jax.numpy as jnp
from jax import lax
from jax.experimental import pallas as pl
from jax.experimental.pallas import tpu as pltpu
from jax.sharding import PartitionSpec as P

DC = 512
DR = 64
DL = 576
DN = 128
DQ = 192
ROWS = 128
KEYS = 256
HEADS = 4
VMEM = 60
FLOPS = 4_000_000_000
SCALE = 1.0 / DQ**0.5
LOG2E = 1.4426950408889634
F32 = jnp.float32
BF16 = jnp.bfloat16


def mm(a, b, ca, cb):
    return lax.dot_general(a, b, (((ca,), (cb,)), ((), ())), preferred_element_type=F32)


def attend_kernel(layout, more, last, order_ref, rows_hbm, mask_hbm, q_hbm, g_hbm, *rest):
    w_hbm = rest[more : more + 1 + max(entry[0] for entry in layout)]
    outs = rest[:-11][-4 if last else -3 :]
    out_ref, dq_ref = outs[:2]
    rows_ref, mask_ref, q_all, g_all, w_all, before_ref, acc_ref, kv_ref, dkv_ref = rest[-11:-2]
    arrived, loaded = rest[-2:]
    step, steps = pl.program_id(0), w_all.shape[0]

    def piece(index):
        source, shard, slot, row = layout[index]
        first = 0 if row is None else pl.multiple_of(order_ref[steps + row], 128)
        ref = w_hbm[source].at[shard]
        return pltpu.make_async_copy(
            ref, w_all.at[slot, pl.ds(first, ref.shape[0])], arrived.at[slot]
        )

    def block(ref, all_ref, slot, number, sem):
        width = all_ref.shape[2]
        columns = pl.ds(pl.multiple_of(order_ref[number] * width, width), width)
        return pltpu.make_async_copy(ref.at[:, columns], all_ref.at[slot], loaded.at[sem])

    rows_copy = pltpu.make_async_copy(rows_hbm, rows_ref, loaded.at[2 * steps])
    mask_copy = pltpu.make_async_copy(mask_hbm, mask_ref, loaded.at[2 * steps + 1])
    if more:
        before_copy = pltpu.make_async_copy(rest[0], before_ref, loaded.at[2 * steps + 2])

    def ask(slot):
        for index, entry in enumerate(layout):
            if entry[2] == slot:
                piece(index).start()
        block(q_hbm, q_all, slot, slot, slot).start()
        block(g_hbm, g_all, slot, slot, steps + slot).start()

    @pl.when(step == 0)
    def _():
        rows_copy.start()
        ask(0)
        mask_copy.start()
        acc_ref[...] = jnp.zeros_like(acc_ref)
        rows_copy.wait()
        mask_copy.wait()

    pltpu.make_async_copy(w_all.at[step], w_all.at[step], arrived.at[step]).wait()
    pltpu.make_async_copy(q_all.at[step], q_all.at[step], loaded.at[step]).wait()
    pltpu.make_async_copy(g_all.at[step], g_all.at[step], loaded.at[steps + step]).wait()

    @pl.when(step == 0)
    def _():
        for slot in range(1, steps):
            ask(slot)
        if more:
            before_copy.start()

    q_ref, g_ref = q_all.at[step], g_all.at[step]
    w = w_all[step]
    kv_ref[...] = mm(rows_ref[:, :DC], w, 1, 0).astype(BF16)
    rope_even = rows_ref[:, DC : DC + 128]
    rope_odd = rows_ref[:, DC + 128 :]
    bias = mask_ref[:ROWS, :]
    alive = mask_ref[ROWS : ROWS + 1, :]
    low = lax.broadcasted_iota(jnp.int32, (KEYS, 128), 1) < DR
    staged = []
    for pair in range(HEADS // 2):
        for odd in range(2):
            head = pair * 2 + odd
            at = pair * 384 + odd * 128
            q = q_ref[:, at : at + 256]
            g = g_ref[:, head * 128 : (head + 1) * 128]
            key = kv_ref[:, head * 256 : head * 256 + 128]
            value = kv_ref[:, head * 256 + 128 : (head + 1) * 256]
            if odd:
                turned = jnp.concatenate([key[:, DR:], key[:, :DR]], axis=1)
                zero = jnp.zeros_like(turned)
                key_row = jnp.concatenate(
                    [jnp.where(low, zero, turned), jnp.where(low, turned, rope_odd)], axis=1
                )
            else:
                key_row = jnp.concatenate([key, rope_even], axis=1)
            s = mm(key_row, q, 1, 1)
            s = jnp.concatenate([s[:ROWS], s[ROWS:] + bias], axis=0)
            d_a = mm(value, g, 1, 1)
            staged.append((q, g, value, key_row, s, d_a))
    for pair in range(HEADS // 2):
        merged = None
        for odd in range(2):
            head = pair * 2 + odd
            q, g, value, key_row, s, d_a = staged[head]
            top = jnp.max(s, axis=0, keepdims=True)
            e = jnp.exp2((s - top) * (SCALE * LOG2E))
            inv = alive / jnp.sum(e, axis=0, keepdims=True)
            a_b = (e * inv).astype(BF16)
            delta = jnp.sum(e * d_a, axis=0, keepdims=True) * inv
            d_s = ((e * (d_a - delta)) * (inv * SCALE)).astype(BF16)
            out_ref[:, head * 128 : (head + 1) * 128] = mm(a_b, value, 0, 0).astype(BF16)
            d_q = mm(d_s, key_row, 0, 0)
            if odd:
                dq_ref[:, pair * 384 : pair * 384 + 128] = merged[:, :128].astype(BF16)
                dq_ref[:, pair * 384 + 128 : pair * 384 + 256] = (
                    merged[:, 128:] + d_q[:, :128]
                ).astype(BF16)
                dq_ref[:, pair * 384 + 256 : pair * 384 + 384] = d_q[:, 128:].astype(BF16)
            else:
                merged = d_q
            d_k = mm(d_s, q, 1, 0)
            d_v = mm(a_b, g, 1, 0)
            if odd:
                d_key = jnp.concatenate([d_k[:, DR:128], d_k[:, 128 : 128 + DR]], axis=1)
                acc_ref[:, DC + 128 :] += d_k[:, 128:]
            else:
                d_key = d_k[:, :128]
                acc_ref[:, DC : DC + 128] += d_k[:, 128:]
            dkv_ref[:, head * 256 : head * 256 + 128] = d_key.astype(BF16)
            dkv_ref[:, head * 256 + 128 : (head + 1) * 256] = d_v.astype(BF16)
    acc_ref[:, :DC] += mm(dkv_ref[...], w, 1, 1)


    @pl.when(step == steps - 1)
    def _():
        total = acc_ref[...]
        if more:
            before_copy.wait()
            total += before_ref[...]
        if last:
            rope_sum = total[:, DC : DC + DR] + total[:, DC + 128 + DR :]
            for ref, rows in zip(outs[2:], (slice(0, ROWS), slice(ROWS, KEYS))):
                ref[:, :DC] = total[rows, :DC].astype(BF16)
                ref[:, DC:] = rope_sum[rows].astype(BF16)
        else:
            outs[2][...] = total


def attend(order, rows, mask, weights, layout, queries, grads, before=(), last=False):
    steps = 1 + max(entry[2] for entry in layout)
    split = lambda i, order: (0, order[i])
    args = [order, rows, mask, queries, grads]
    args += list(before[2:]) + list(weights) + list(before[:2])
    aliases = {len(args) - 2: 0, len(args) - 1: 1} if before else {}
    results = [jax.ShapeDtypeStruct((KEYS, 768), F32)]
    if last:
        results = [jax.ShapeDtypeStruct((ROWS, DL), BF16)] * 2
    return pl.pallas_call(
        functools.partial(attend_kernel, layout, int(bool(before)), last),
        grid_spec=pltpu.PrefetchScalarGridSpec(
            num_scalar_prefetch=1,
            grid=(steps,),
            in_specs=[pl.BlockSpec(memory_space=pl.ANY)] * (len(args) - 1),
            out_specs=[
                pl.BlockSpec((ROWS, 512), split),
                pl.BlockSpec((ROWS, 768), split),
            ]
            + [pl.BlockSpec(result.shape, lambda i, order: (0, 0)) for result in results],
            scratch_shapes=[
                pltpu.VMEM((KEYS, 768), BF16),
                pltpu.VMEM((ROWS + 8, 128), F32),
                pltpu.VMEM((steps, ROWS, 768), BF16),
                pltpu.VMEM((steps, ROWS, 512), BF16),
                pltpu.VMEM((steps, DC, 1024), BF16),
                pltpu.VMEM((KEYS, 768), F32),
                pltpu.VMEM((KEYS, 768), F32),
                pltpu.VMEM((KEYS, 1024), BF16),
                pltpu.VMEM((KEYS, 1024), BF16),
                pltpu.SemaphoreType.DMA((steps,)),
                pltpu.SemaphoreType.DMA((2 * steps + 3,)),
            ],
        ),
        out_shape=[
            jax.ShapeDtypeStruct((ROWS, 8192), BF16),
            jax.ShapeDtypeStruct((ROWS, 12288), BF16),
        ]
        + results,
        input_output_aliases=aliases,
        compiler_params=pltpu.CompilerParams(vmem_limit_bytes=VMEM * 1024 * 1024),
        cost_estimate=pl.CostEstimate(
            flops=steps * FLOPS, bytes_accessed=steps * 1_800_000, transcendentals=0
        ),
    )(*args)


def at(x, y, z, core):
    return ((z % 8) * 2 + core) * 16 + (x % 4) * 4 + y % 4


CHIPS = [(x, y, z) for x in range(4) for y in range(4) for z in range(8)]
SWAP = [(at(x, y, z, c), at(x, y, z, 1 - c)) for x, y, z in CHIPS for c in range(2)]


RING = [(at(x, y, z, 0), at(x, y, z + 1, 0)) for x, y, z in CHIPS] + [
    (at(x, y, z, 1), at(x, y, z - 1, 1)) for x, y, z in CHIPS
]
PLANE = [(at(x, y, z, 0), at(x + 1, y, z, 0)) for x, y, z in CHIPS] + [
    (at(x, y, z, 1), at(x, y + 1, z, 1)) for x, y, z in CHIPS
]


def send(a, pairs):
    return lax.ppermute(a, ("prompt", "sample"), pairs)


def places():
    prompt, sample = lax.axis_index("prompt"), lax.axis_index("sample")
    z, core = prompt // 2, prompt % 2
    x, y = sample // 4, sample % 4
    mine = jnp.where(core == 0, x, y)
    other = jnp.where(core == 0, y, x)
    return z, core, mine, other


def after(a, *done):
    return lax.optimization_barrier((a,) + done)[0]


def around(piece):
    local = [piece, send(piece, PLANE)]
    return local + [send(part, SWAP) for part in local]


def layout_of(source, slot, shards):
    return tuple(
        (source + 2 * way + part, shard, slot + way * shards + shard, 2 * way + part)
        for way in (0, 1)
        for shard in range(shards)
        for part in (0, 1)
    )


def body(prompt_latent, resp_latent, queries, d_attended, w_kv, seg_ids, live):
    z, core, mine, other = places()
    prompt = 2 * z + core
    half, other_half = mine % 2 * 256, other % 2 * 256
    pair = [w_kv, send(w_kv, SWAP)]
    here = jnp.stack([lax.dynamic_slice_in_dim(w, half, 256, 0) for w in pair])
    ring = send(here, RING)
    pair = [w[None] for w in pair]
    whole_prompt = lax.all_to_all(
        jnp.tile(after(prompt_latent, here).reshape(-1, DL), (16, 1)), "sample", 0, 0, tiled=True
    )
    rows = jnp.concatenate([whole_prompt, resp_latent.reshape(-1, DL)], axis=0)
    blank = jnp.zeros((KEYS, 128), BF16)
    rows = jnp.concatenate([rows, blank, rows[:, DC:]], axis=1)
    seg = seg_ids[0]
    position = jnp.arange(ROWS, dtype=jnp.int32)
    seen = (
        (seg[:, None] == seg[None, :])
        & (position[:, None] <= position[None, :])
        & (position[:, None] < live[0, 0])
    )
    bias = jnp.where(seen, F32(0.0), F32(-1e30))
    alive = (position < live[0, 0]).astype(F32)[None, :]
    mask = jnp.concatenate([bias, jnp.broadcast_to(alive, (8, ROWS))], axis=0)
    ring, rows, mask = lax.optimization_barrier((ring, rows, mask))
    tensors = (queries[0], d_attended[0])
    starts = jnp.stack([half, 256 - half, other_half, 256 - other_half])
    way = 2 * core - 1

    def order(*steps):
        numbers = []
        for step in steps:
            if step in (0, 4):
                numbers += [2 * ((z + step) % 8) + core, 2 * ((z + step) % 8) + 1 - core]
            else:
                near, far = 2 * ((z + way * step) % 8), 2 * ((z - way * step) % 8)
                numbers += [near + core, near + 1 - core, far + 1 - core, far + core]
        return jnp.concatenate([jnp.stack(numbers), starts]).astype(jnp.int32)

    pair_layout = ((0, 0, 0, None), (1, 0, 1, None))
    results = attend(
        order(0, 1), rows, mask, pair + around(ring), pair_layout + layout_of(2, 2, 2), *tensors
    )
    ring = send(ring, RING)
    second = around(ring)
    ring, before = lax.optimization_barrier((send(ring, RING), results[2]))
    attended, d_queries, prompt_term, resp_term = attend(
        order(2, 3, 4), rows, mask, second + around(ring) + around(send(ring[:1], RING)),
        layout_of(0, 0, 2) + layout_of(4, 4, 2) + layout_of(8, 8, 1),
        *tensors, [*results[:2], before], last=True,
    )
    pieces = lax.all_to_all(prompt_term, "sample", 0, 0, tiled=True).reshape(16, -1, DL)
    d_prompt = jnp.sum(pieces.astype(F32), axis=0).astype(BF16).reshape(1, -1)
    d_resp = resp_term.reshape(1, -1)
    return (attended[None], d_queries[None], d_prompt, d_resp)


def solution(mesh):
    rows = P("prompt", "sample")
    wide = P("prompt", "sample", None)
    return jax.shard_map(
        body,
        mesh=mesh,
        in_specs=(rows, rows, wide, wide, P(None, "prompt"), rows, rows),
        out_specs=(wide, wide, rows, rows),
        check_vma=False,
    )
```
